128 devices in a mesh: row: 8 (over y, core), col: 16 (over x, z).
Axes of the slice: x: 4, y: 4, z: 4, core: 2. Of those that a mesh axis runs over, the one named last changes fastest.
Arguments:
- lower_blocks: float32 [6, 1024, 1024], P(None, 'col', 'row'), may hold values from -0.125 to 0.125
- inverses: float32 [4, 1024, 1024], P(None, 'col', 'row'), may hold values from -0.0625 to 1.5, as said below
- panel_right: float32 [4, 1024, 1024], P(None, 'row'), may hold values from -6 to 6
- trail_factor: float32 [4, 1024, 65536], P(None, 'col', 'row'), may hold values from -0.125 to 0.125
- trail_right: float32 [65536, 1024], P(('row', 'col')), may hold values from -6 to 6
Outputs:
- solution: float32 [4, 1024, 1024], P(None, 'col', 'row')
- updated: float32 [65536, 1024], P(('row', 'col'))
The draws below stay inside these ranges and needn't reach their ends.
Inputs may be any that keep to these rules, and one draw needn't show every extreme that they name: inverses holds float32 matrices with diagonal entries between 0.5 and 1.5.
All inputs are finite; a program needn't handle non-finite values.
Results may differ from the reference program's by a relative error of at most 0.00011.
Values sent between devices are 32-bit elements; how exact they have to be, the bound alone decides.
No kernel may reach another device: no remote copies, remote signals or barrier semaphores. Data moves between devices by JAX's collectives and lax.ppermute only.
A program may use at most 192 MiB of HBM per device.

```python
import jax
import jax.numpy as jnp
from jax import lax

BLK = 1024
STEPS = 4
QCOLS = 1024
PAIRS = 6
TRAIL = 65536


def draw_inverses(key, part):
    key = jax.random.fold_in(key, 7)
    first, second = jax.random.split(key, 2)
    shape = (STEPS, BLK, BLK)
    eye_mask = (lax.broadcasted_iota(jnp.int32, shape, 1) == lax.broadcasted_iota(jnp.int32, shape, 2)).astype(jnp.float32)
    diagonal = jax.random.uniform(first, shape, jnp.float32, 0.6, 1.4)
    spread = jnp.clip(jax.random.normal(second, shape, jnp.float32), -4.0, 4.0) * (0.5 * BLK ** (-0.5))
    return eye_mask * diagonal + (1.0 - eye_mask) * spread


def spiked(array, key, source, target, blocks, factor):
    def block_of(position):
        return (jnp.arange(array.shape[position]) // (array.shape[position] // blocks)).reshape((-1,) + (1,) * (array.ndim - 1 - position))

    first = jax.random.permutation(key, blocks)[block_of(target)]
    second = (block_of(target) + blocks // 2) % blocks
    return jnp.where((block_of(source) == first) | (block_of(source) == second), factor * array, array)


def block_levels(key, extent, shards, low, top_value):
    def one(position, shards_of):
        steps = jax.random.uniform(jax.random.fold_in(jax.random.fold_in(key, 6), position), (shards_of,), jnp.float32, low / len(shards), top_value / len(shards))
        return jnp.repeat(jnp.exp(steps), extent[position] // shards_of).reshape((-1,) + (1,) * (len(extent) - position - 1))

    gain = one(*shards[0])
    for cut in shards[1:]:
        gain = gain * one(*cut)
    return gain


def normal_values(rng, dims, deviation, most, cuts=(), dtype=jnp.bfloat16):
    drawn = deviation * jax.random.normal(rng, dims, jnp.float32)
    if cuts:
        drawn = drawn * block_levels(rng, dims, cuts, -0.22, 0.18)
    return jnp.clip(drawn, -most, most).astype(dtype)


def heavy_noise(rng, extent, scale, reach, pieces, heavy, kind=jnp.bfloat16):
    drawn = scale * jax.random.normal(rng, extent, jnp.float32)
    if pieces:
        drawn = drawn * block_levels(rng, extent, pieces, -0.22, 0.18)
    return jnp.clip(spiked(drawn, jax.random.fold_in(rng, 3), *heavy), -reach, reach).astype(kind)


def setup_inputs(seed: int = 0) -> dict:
    seeds = jax.random.split(jax.random.key(seed), 6)
    lower_blocks = normal_values(seeds[0], (PAIRS, BLK, BLK), (2 * BLK) ** -0.5, 0.125, ((1, 16), (2, 8)), jnp.float32)
    inverses = draw_inverses(jax.random.fold_in(seeds[5], 71), 0)
    panel_right = normal_values(seeds[2], (STEPS, BLK, QCOLS), 1.0, 6.0, ((1, 8),), jnp.float32)
    trail_factor = heavy_noise(seeds[3], (STEPS, BLK, TRAIL), (STEPS * BLK) ** -0.5, 0.125, ((1, 16), (2, 8)), (1, 2, 16, 2.0), jnp.float32)
    trail_right = normal_values(seeds[4], (TRAIL, QCOLS), 1.0, 6.0, ((0, 128),), jnp.float32)
    return dict(lower_blocks=lower_blocks, inverses=inverses, panel_right=panel_right, trail_factor=trail_factor, trail_right=trail_right)


def first_contract(left, right):
    return lax.dot_general(left, right, (((0,), (0,)), ((), ())), precision=lax.Precision.HIGHEST, preferred_element_type=jnp.float32)


def reference(lower_blocks, inverses, panel_right, trail_factor, trail_right):
    highest = lax.Precision.HIGHEST
    solved = []
    for step in range(STEPS):
        remaining = panel_right[step]
        for prior in range(step):
            index = step * (step - 1) // 2 + prior
            remaining = remaining - first_contract(lower_blocks[index], solved[prior])
        solved.append(jnp.dot(inverses[step], remaining, precision=highest, preferred_element_type=jnp.float32))
    solution = jnp.stack(solved)
    flat_factor = trail_factor.reshape(STEPS * BLK, TRAIL)
    product = first_contract(flat_factor, solution.reshape(STEPS * BLK, QCOLS))
    return solution, trail_right - product
```

```python
import jax
import jax.numpy as jnp
from jax import lax
from jax.experimental import pallas as pl
from jax.experimental.pallas import tpu as pltpu
from jax.sharding import PartitionSpec as P

F32 = jnp.float32
BF16 = jnp.bfloat16


def col_perm(dx, dz):
    return [(((x + dx) % 4) * 4 + (z + dz) % 4, x * 4 + z) for x in range(4) for z in range(4)]


def y_perm(dy):
    return [(2 * ((y + dy) % 4) + c, 2 * y + c) for y in range(4) for c in range(2)]


CORE_PERM = [(i, i ^ 1) for i in range(8)]


def from_x(value, d):
    return lax.ppermute(value, "col", col_perm(d, 0))


def from_z(value, d):
    return lax.ppermute(value, "col", col_perm(0, d))


def from_y(value, d):
    return lax.ppermute(value, "row", y_perm(d))


def from_core(value):
    return lax.ppermute(value, "row", CORE_PERM)


def ring_stack(value, fetch):
    far = {d: fetch(value, d) for d in (1, 3, 2)}
    return jnp.stack([value, far[1], far[2], far[3]])


def gather_blocks(set_a, set_b):
    near_a = ring_stack(set_a, from_x)
    near_b = ring_stack(set_b, from_z)
    near_a, near_b = lax.optimization_barrier((near_a, near_b))
    all_a = jnp.swapaxes(ring_stack(near_a, from_z), 0, 1)
    all_b = ring_stack(near_b, from_x)
    return all_a.reshape((-1,) + set_a.shape), all_b.reshape((-1,) + set_b.shape)


def split_bf16(value):
    high = value.astype(BF16)
    low = (value - high.astype(F32)).astype(BF16)
    return high, low


def dot3(a, b, dims):
    ah, al = split_bf16(a)
    bh, bl = split_bf16(b)

    def one(p, q):
        return lax.dot_general(p, q, (dims, ((), ())), preferred_element_type=F32)

    return one(ah, bh) + (one(ah, bl) + one(al, bh))


def dot_nn(a, b):
    return dot3(a, b, ((1,), (0,)))


def dot_nt(a, b):
    return dot3(a, b, ((1,), (1,)))


def flat(ref):
    value = ref[:, 0]
    return value.reshape(value.shape[0] * value.shape[1], value.shape[2])


def take_piece(place_ref, piece_ref, total):
    x, y, z = place_ref[0], place_ref[1], place_ref[2]
    width = piece_ref.shape[1]
    shift = lax.rem(y - x + 4, 4)
    quarter = total[:, 0:width]
    for d in range(1, 4):
        quarter = jnp.where(shift == d, total[:, d * width:(d + 1) * width], quarter)
    piece_ref[...] = pltpu.roll(quarter, z * (width // 4), 1)


def first_step_kernel(rem_ref, inv_own, inv_far, part_ref):
    half = inv_own.shape[3]
    rem = rem_ref[0]
    part_ref[...] = dot_nt(rem[:, :half], flat(inv_own)) + dot_nt(rem[:, half:], flat(inv_far))


def step_kernel(place_ref, p0, p1, p2, p3, rem_ref, low_own, low_far, inv_own, inv_far, x_ref, piece_ref, part_ref):
    half = inv_own.shape[3]
    total = (p0[...] + p1[...]) + (p2[...] + p3[...])
    x_ref[...] = total
    take_piece(place_ref, piece_ref, total)
    rem = rem_ref[0]
    left = rem[:, :half] - dot_nn(total, flat(low_own))
    right = rem[:, half:] - dot_nn(total, flat(low_far))
    part_ref[...] = dot_nt(left, flat(inv_own)) + dot_nt(right, flat(inv_far))


def last_step_kernel(place_ref, p0, p1, p2, p3, piece_ref):
    take_piece(place_ref, piece_ref, (p0[...] + p1[...]) + (p2[...] + p3[...]))


def ahead_kernel(x_ref, rem_ref, low_own, low_far, o_ref):
    half = low_own.shape[3]
    total = x_ref[...]
    o_ref[0, :, :half] = rem_ref[0, :, :half] - dot_nn(total, flat(low_own))
    o_ref[0, :, half:] = rem_ref[0, :, half:] - dot_nn(total, flat(low_far))


def block_spec(place):
    where, index = place
    shape = where.shape
    return pl.BlockSpec((shape[0], 1) + shape[2:], lambda *_: (0, index, 0, 0))


def whole_spec(array):
    zeros = (0,) * len(array.shape)
    return pl.BlockSpec(array.shape, lambda *_: zeros)


def small_call(kernel, place, plain, blocks, outs):
    specs = [whole_spec(v) for v in plain] + [block_spec(v) for v in blocks]
    return pl.pallas_call(
        kernel,
        grid_spec=pltpu.PrefetchScalarGridSpec(
            num_scalar_prefetch=0 if place is None else 1,
            grid=(1,),
            in_specs=specs,
            out_specs=[whole_spec(v) for v in outs],
        ),
        out_shape=outs,
        compiler_params=pltpu.CompilerParams(vmem_limit_bytes=40 * 2**20),
    )(*([] if place is None else [place]), *plain, *[v[0] for v in blocks])


def split_kernel(f_ref, o_ref):
    parts = o_ref.shape[0]
    width = o_ref.shape[3]
    for d in range(parts):
        o_ref[d, 0] = f_ref[0, :, d * width:(d + 1) * width]


def split_by_owner(factor, first, count, owners):
    rows = factor.shape[1]
    width = factor.shape[2] // owners
    per = 4
    return pl.pallas_call(
        split_kernel,
        grid=(count, owners // per),
        in_specs=[pl.BlockSpec((1, rows, per * width), lambda k, g: (first + k, 0, g))],
        out_specs=pl.BlockSpec((per, 1, rows, width), lambda k, g: (g, k, 0, 0)),
        out_shape=jax.ShapeDtypeStruct((owners, count, rows, width), F32),
        compiler_params=pltpu.CompilerParams(vmem_limit_bytes=32 * 2**20),
    )(factor)


def dot_b(a, b):
    return lax.dot_general(a, b, (((1,), (1,)), ((), ())), preferred_element_type=F32)


def update_kernel(place_ref, f_ref, *refs):
    x_refs = refs[:8]
    base_ref, o_ref, s_ref, high_ref, low_ref = refs[8:]
    step = pl.program_id(0)
    x, y, z, core, row = [place_ref[i] for i in range(5)]
    half = o_ref.shape[1] // 2
    width = x_refs[0].shape[3]

    @pl.when(step == 0)
    def _():
        o_ref[...] = base_ref[...]

    for d in range(4):
        quarter = pl.ds(pl.multiple_of(lax.rem(y + d, 4) * width, width), width)
        for side in range(2):
            part = x_refs[2 * d + side][:, 0]
            part = part.reshape(part.shape[0] * part.shape[1], width)
            high, low = split_bf16(part)
            high_ref[side, :, quarter] = high
            low_ref[side, :, quarter] = low

    block = s_ref.shape[1]
    for d in range(4):
        for side in range(2):
            mine = (lax.rem(x - y + 4, 4) == d) & ((row // 4 == core) == (side == 0))

            @pl.when(mine)
            def _(part_ref=x_refs[2 * d + side]):
                part = part_ref[pl.ds(4 * lax.rem(row, 4), 4), 0]
                part = part.reshape(part.shape[0] * part.shape[1], width)
                part = pltpu.roll(part, lax.rem(4 - z, 4) * block, 1)
                s_ref[0] = part[:, :128].T[:block]

    f = f_ref[:, 0]
    f = f.reshape(f.shape[0] * f.shape[1], f.shape[2]).T
    fh, fl = split_bf16(f)
    for side in range(2):
        where = core if side == 0 else 1 - core
        cols = pl.ds(pl.multiple_of(where * half, half), half)
        xh = high_ref[side]
        o_ref[:, cols] -= dot_b(fh, xh) + (dot_b(fh, low_ref[side]) + dot_b(fl, xh))


def update(place, factor, f_first, xs, x_first, count, base, s_rows, s_cols):
    owners, _, rows, width = factor.shape
    _, _, q, m = xs[0].shape
    whole = pl.BlockSpec(base.shape, lambda k, p: (0, 0))
    grid_spec = pltpu.PrefetchScalarGridSpec(
        num_scalar_prefetch=1,
        grid=(count,),
        in_specs=[pl.BlockSpec((owners, 1, rows, width), lambda k, p: (0, f_first + k, 0, 0))]
        + [pl.BlockSpec((owners, 1, q, m), lambda k, p: (0, x_first + k, 0, 0))] * 8
        + [whole],
        out_specs=[whole, pl.BlockSpec((1, s_rows, s_cols), lambda k, p: (k, 0, 0))],
        scratch_shapes=[
            pltpu.VMEM((2, owners * q, 4 * m), BF16),
            pltpu.VMEM((2, owners * q, 4 * m), BF16),
        ],
    )
    return pl.pallas_call(
        update_kernel,
        grid_spec=grid_spec,
        out_shape=[
            jax.ShapeDtypeStruct(base.shape, F32),
            jax.ShapeDtypeStruct((count, s_rows, s_cols), F32),
        ],
        compiler_params=pltpu.CompilerParams(vmem_limit_bytes=56 * 2**20),
    )(place, factor, *xs, base)


def per_device(lower_blocks, inverses, panel_right, trail_factor, trail_right):
    row = lax.axis_index("row")
    col = lax.axis_index("col")
    y, core = row // 2, row % 2
    x, z = col // 4, col % 4

    place = jnp.stack([x, y, z, core, row]).astype(jnp.int32)
    steps = inverses.shape[0]
    order = inverses.shape[1] * 16
    q_all = panel_right.shape[2]
    share = q_all // 32

    def columns(which):
        return lax.dynamic_slice_in_dim(panel_right, which * (q_all // 2) + col * share, share, 2)

    right_own = jnp.swapaxes(columns(core), 1, 2)
    right_far = from_core(jnp.swapaxes(columns(1 - core), 1, 2))
    right = jnp.concatenate([right_own, right_far], axis=2)

    set_a = jnp.concatenate([inverses[0:1], lower_blocks[0:1], inverses[1:2], lower_blocks[1:3]])
    set_b = jnp.concatenate([inverses[2:4], lower_blocks[3:6]])
    got_a, got_b = gather_blocks(set_a, set_b)
    far_a = from_core(got_a)
    far_b = from_core(got_b)
    inv = [(0, 0), (0, 2), (1, 0), (1, 1)]
    low = {(1, 0): (0, 1), (2, 0): (0, 3), (2, 1): (0, 4), (3, 0): (1, 2), (3, 1): (1, 3), (3, 2): (1, 4)}

    def both(where):
        pair = ((got_a, far_a), (got_b, far_b))[where[0]]
        return [(v, where[1]) for v in pair]

    split_0 = split_by_owner(trail_factor, 0, 1, 16)
    split_1 = split_by_owner(trail_factor, 1, 1, 16)
    split_2 = split_by_owner(trail_factor, 2, 2, 16)

    def after(value, *earlier):
        return lax.optimization_barrier((value,) + earlier)[0]

    factor_0 = lax.all_to_all(after(split_0, got_a, got_b, split_1, split_2), "col", 0, 0)

    x_shape = jax.ShapeDtypeStruct((share, order), F32)
    piece_shape = jax.ShapeDtypeStruct((share, order // 4), F32)
    rem_shape = jax.ShapeDtypeStruct((1, share, right.shape[2]), F32)
    rem = [right[k:k + 1] for k in range(steps)]

    pieces = []
    (part,) = small_call(first_step_kernel, None, [rem[0]], both(inv[0]), [x_shape])
    for k in range(1, steps + 1):
        parts = [part] + [from_y(part, d) for d in (1, 3, 2)]
        if k == steps:
            (piece,) = small_call(last_step_kernel, place, parts, [], [piece_shape])
        else:
            solved, piece, part = small_call(
                step_kernel, place, parts + [rem[k]], both(low[(k, k - 1)]) + both(inv[k]),
                [x_shape, piece_shape, x_shape],
            )
            for later in range(k + 1, steps):
                (rem[later],) = small_call(ahead_kernel, None, [solved, rem[later]], both(low[(later, k - 1)]), [rem_shape])
        pieces.append(piece)

    def spread(two):
        return jnp.broadcast_to(jnp.stack(two)[None], (16, 2) + two[0].shape)

    def core_pairs(parts):
        out = []
        for part in parts:
            out += [part, from_core(part)]
        return out

    block = (inverses.shape[1], inverses.shape[2])
    x_01 = lax.all_to_all(after(spread(pieces[0:2]), factor_0), "col", 0, 0)
    factor_1 = lax.all_to_all(after(split_1, x_01), "col", 0, 0)
    up_01, down_01 = from_y(x_01, 1), from_y(x_01, 3)
    x_23 = lax.all_to_all(after(spread(pieces[2:4]), factor_1, up_01, down_01), "col", 0, 0)
    across_01 = from_y(after(x_01, up_01, down_01), 2)
    factor_2 = lax.all_to_all(after(split_2, x_23), "col", 0, 0)
    xs_01 = core_pairs([x_01, up_01, across_01, down_01])
    out, solved_0 = update(place, factor_0, 0, xs_01, 0, 1, trail_right, *block)
    out, solved_1 = update(place, factor_1, 0, xs_01, 1, 1, out, *block)
    x_23 = after(x_23, across_01)
    up_23, down_23 = from_y(x_23, 1), from_y(x_23, 3)
    across_23 = from_y(after(x_23, out, up_23, down_23), 2)
    xs_23 = core_pairs([x_23, up_23, across_23, down_23])
    out, solved_2 = update(place, factor_2, 0, xs_23, 0, 2, out, *block)
    return (jnp.concatenate([solved_0, solved_1, solved_2]), out)


def solution(mesh):
    in_specs = (
        P(None, "col", "row"),
        P(None, "col", "row"),
        P(None, "row", None),
        P(None, "col", "row"),
        P(("row", "col"), None),
    )
    out_specs = (P(None, "col", "row"), P(("row", "col"), None))
    return jax.shard_map(
        per_device, mesh=mesh, in_specs=in_specs, out_specs=out_specs, check_vma=False
    )
```

```python
import jax
import jax.numpy as jnp
from jax import lax
from jax.experimental import pallas as pl
from jax.experimental.pallas import tpu as pltpu
from jax.sharding import PartitionSpec as P

F32 = jnp.float32
BF16 = jnp.bfloat16


def col_perm(dx, dz):
    return [(((x + dx) % 4) * 4 + (z + dz) % 4, x * 4 + z) for x in range(4) for z in range(4)]


def y_perm(dy):
    return [(2 * ((y + dy) % 4) + c, 2 * y + c) for y in range(4) for c in range(2)]


CORE_PERM = [(i, i ^ 1) for i in range(8)]


def from_x(value, d):
    return lax.ppermute(value, "col", col_perm(d, 0))


def from_z(value, d):
    return lax.ppermute(value, "col", col_perm(0, d))


def from_y(value, d):
    return lax.ppermute(value, "row", y_perm(d))


def from_core(value):
    return lax.ppermute(value, "row", CORE_PERM)


def ring_stack(value, fetch):
    far = {d: fetch(value, d) for d in (1, 3, 2)}
    return jnp.stack([value, far[1], far[2], far[3]])


def gather_blocks(set_a, set_b, *others):
    near_a = ring_stack(set_a, from_x)
    near_b = ring_stack(set_b, from_z)
    near_a, near_b, *others = lax.optimization_barrier((near_a, near_b) + others)
    all_a = jnp.swapaxes(ring_stack(near_a, from_z), 0, 1)
    all_b = ring_stack(near_b, from_x)
    return all_a.reshape((-1,) + set_a.shape), all_b.reshape((-1,) + set_b.shape), *others


def split_bf16(value):
    high = value.astype(BF16)
    low = (value - high.astype(F32)).astype(BF16)
    return high, low


def dot3(a, b, dims):
    ah, al = split_bf16(a)
    bh, bl = split_bf16(b)

    def one(p, q):
        return lax.dot_general(p, q, (dims, ((), ())), preferred_element_type=F32)

    return one(ah, bh) + (one(ah, bl) + one(al, bh))


def dot_nn(a, b):
    return dot3(a, b, ((1,), (0,)))


def dot_nt(a, b):
    return dot3(a, b, ((1,), (1,)))


def flat(ref):
    value = ref[:, 0]
    return value.reshape(value.shape[0] * value.shape[1], value.shape[2])


def take_piece(place_ref, piece_ref, total):
    x, y, z = place_ref[0], place_ref[1], place_ref[2]
    width = piece_ref.shape[1]
    shift = lax.rem(y - x + 4, 4)
    quarter = total[:, 0:width]
    for d in range(1, 4):
        quarter = jnp.where(shift == d, total[:, d * width:(d + 1) * width], quarter)
    piece_ref[...] = pltpu.roll(quarter, z * (width // 4), 1)


def first_step_kernel(rem_ref, inv_own, inv_far, part_ref):
    half = inv_own.shape[3]
    rem = rem_ref[0]
    part_ref[...] = dot_nt(rem[:, :half], flat(inv_own)) + dot_nt(rem[:, half:], flat(inv_far))


def step_kernel(place_ref, p0, p1, p2, p3, rem_ref, low_own, low_far, inv_own, inv_far, x_ref, piece_ref, part_ref):
    half = inv_own.shape[3]
    total = (p0[...] + p1[...]) + (p2[...] + p3[...])
    x_ref[...] = total
    take_piece(place_ref, piece_ref, total)
    rem = rem_ref[0]
    left = rem[:, :half] - dot_nn(total, flat(low_own))
    right = rem[:, half:] - dot_nn(total, flat(low_far))
    part_ref[...] = dot_nt(left, flat(inv_own)) + dot_nt(right, flat(inv_far))


def last_step_kernel(place_ref, p0, p1, p2, p3, piece_ref):
    take_piece(place_ref, piece_ref, (p0[...] + p1[...]) + (p2[...] + p3[...]))


def ahead_kernel(x_ref, rem_ref, low_own, low_far, o_ref):
    half = low_own.shape[3]
    total = x_ref[...]
    o_ref[0, :, :half] = rem_ref[0, :, :half] - dot_nn(total, flat(low_own))
    o_ref[0, :, half:] = rem_ref[0, :, half:] - dot_nn(total, flat(low_far))


def block_spec(place):
    where, index = place
    shape = where.shape
    return pl.BlockSpec((shape[0], 1) + shape[2:], lambda *_: (0, index, 0, 0))


def whole_spec(array):
    zeros = (0,) * len(array.shape)
    return pl.BlockSpec(array.shape, lambda *_: zeros)


def small_call(kernel, place, plain, blocks, outs):
    specs = [whole_spec(v) for v in plain] + [block_spec(v) for v in blocks]
    return pl.pallas_call(
        kernel,
        grid_spec=pltpu.PrefetchScalarGridSpec(
            num_scalar_prefetch=0 if place is None else 1,
            grid=(1,),
            in_specs=specs,
            out_specs=[whole_spec(v) for v in outs],
        ),
        out_shape=outs,
        compiler_params=pltpu.CompilerParams(vmem_limit_bytes=40 * 2**20),
    )(*([] if place is None else [place]), *plain, *[v[0] for v in blocks])


def split_kernel(f_ref, o_ref):
    parts = o_ref.shape[0]
    width = o_ref.shape[3]
    for d in range(parts):
        o_ref[d, 0] = f_ref[0, :, d * width:(d + 1) * width]


def split_by_owner(factor, first, count, owners):
    rows = factor.shape[1]
    width = factor.shape[2] // owners
    per = 4
    return pl.pallas_call(
        split_kernel,
        grid=(count, owners // per),
        in_specs=[pl.BlockSpec((1, rows, per * width), lambda k, g: (first + k, 0, g))],
        out_specs=pl.BlockSpec((per, 1, rows, width), lambda k, g: (g, k, 0, 0)),
        out_shape=jax.ShapeDtypeStruct((owners, count, rows, width), F32),
        compiler_params=pltpu.CompilerParams(vmem_limit_bytes=32 * 2**20),
    )(factor)


def dot_b(a, b):
    return lax.dot_general(a, b, (((1,), (1,)), ((), ())), preferred_element_type=F32)


def update_kernel(place_ref, f_ref, *refs):
    x_refs = refs[:8]
    base_ref, o_ref, s_ref, high_ref, low_ref = refs[8:]
    step = pl.program_id(0)
    x, y, z, core, row = [place_ref[i] for i in range(5)]
    half = o_ref.shape[1] // 2
    width = x_refs[0].shape[3]

    @pl.when(step == 0)
    def _():
        o_ref[...] = base_ref[...]

    for d in range(4):
        quarter = pl.ds(pl.multiple_of(lax.rem(y + d, 4) * width, width), width)
        for side in range(2):
            part = x_refs[2 * d + side][:, 0]
            part = part.reshape(part.shape[0] * part.shape[1], width)
            high, low = split_bf16(part)
            high_ref[side, :, quarter] = high
            low_ref[side, :, quarter] = low

    block = s_ref.shape[1]
    for d in range(4):
        for side in range(2):
            mine = (lax.rem(x - y + 4, 4) == d) & ((row // 4 == core) == (side == 0))

            @pl.when(mine)
            def _(part_ref=x_refs[2 * d + side]):
                part = part_ref[pl.ds(4 * lax.rem(row, 4), 4), 0]
                part = part.reshape(part.shape[0] * part.shape[1], width)
                part = pltpu.roll(part, lax.rem(4 - z, 4) * block, 1)
                s_ref[0] = part[:, :128].T[:block]

    f = f_ref[:, 0]
    f = f.reshape(f.shape[0] * f.shape[1], f.shape[2]).T
    fh, fl = split_bf16(f)
    for side in range(2):
        where = core if side == 0 else 1 - core
        cols = pl.ds(pl.multiple_of(where * half, half), half)
        xh = high_ref[side]
        o_ref[:, cols] -= dot_b(fh, xh) + (dot_b(fh, low_ref[side]) + dot_b(fl, xh))


def update(place, factor, f_first, xs, x_first, count, base, s_rows, s_cols):
    owners, _, rows, width = factor.shape
    _, _, q, m = xs[0].shape
    whole = pl.BlockSpec(base.shape, lambda k, p: (0, 0))
    grid_spec = pltpu.PrefetchScalarGridSpec(
        num_scalar_prefetch=1,
        grid=(count,),
        in_specs=[pl.BlockSpec((owners, 1, rows, width), lambda k, p: (0, f_first + k, 0, 0))]
        + [pl.BlockSpec((owners, 1, q, m), lambda k, p: (0, x_first + k, 0, 0))] * 8
        + [whole],
        out_specs=[whole, pl.BlockSpec((1, s_rows, s_cols), lambda k, p: (k, 0, 0))],
        scratch_shapes=[
            pltpu.VMEM((2, owners * q, 4 * m), BF16),
            pltpu.VMEM((2, owners * q, 4 * m), BF16),
        ],
    )
    return pl.pallas_call(
        update_kernel,
        grid_spec=grid_spec,
        out_shape=[
            jax.ShapeDtypeStruct(base.shape, F32),
            jax.ShapeDtypeStruct((count, s_rows, s_cols), F32),
        ],
        compiler_params=pltpu.CompilerParams(vmem_limit_bytes=56 * 2**20),
    )(place, factor, *xs, base)


def per_device(lower_blocks, inverses, panel_right, trail_factor, trail_right):
    row = lax.axis_index("row")
    col = lax.axis_index("col")
    y, core = row // 2, row % 2
    x, z = col // 4, col % 4

    place = jnp.stack([x, y, z, core, row]).astype(jnp.int32)
    steps = inverses.shape[0]
    order = inverses.shape[1] * 16
    q_all = panel_right.shape[2]
    share = q_all // 32

    def columns(which):
        return lax.dynamic_slice_in_dim(panel_right, which * (q_all // 2) + col * share, share, 2)

    right_own = jnp.swapaxes(columns(core), 1, 2)
    right_far = from_core(jnp.swapaxes(columns(1 - core), 1, 2))
    right = jnp.concatenate([right_own, right_far], axis=2)

    set_a = jnp.concatenate([inverses[0:1], lower_blocks[0:1], inverses[1:2], lower_blocks[1:3]])
    set_b = jnp.concatenate([inverses[2:4], lower_blocks[3:6]])
    split_0 = split_by_owner(trail_factor, 0, 2, 16)
    split_2 = split_by_owner(trail_factor, 2, 2, 16)
    got_a, got_b, right, split_0 = gather_blocks(set_a, set_b, right, split_0)
    far_a = from_core(got_a)
    far_b = from_core(got_b)
    inv = [(0, 0), (0, 2), (1, 0), (1, 1)]
    low = {(1, 0): (0, 1), (2, 0): (0, 3), (2, 1): (0, 4), (3, 0): (1, 2), (3, 1): (1, 3), (3, 2): (1, 4)}

    def both(where):
        pair = ((got_a, far_a), (got_b, far_b))[where[0]]
        return [(v, where[1]) for v in pair]

    def after(value, *earlier):
        return lax.optimization_barrier((value,) + earlier)[0]

    factor_01 = lax.all_to_all(after(split_0, got_a, got_b), "col", 0, 0)

    x_shape = jax.ShapeDtypeStruct((share, order), F32)
    piece_shape = jax.ShapeDtypeStruct((share, order // 4), F32)
    rem_shape = jax.ShapeDtypeStruct((1, share, right.shape[2]), F32)
    rem = [right[k:k + 1] for k in range(steps)]

    pieces = []
    (part,) = small_call(first_step_kernel, None, [rem[0]], both(inv[0]), [x_shape])
    for k in range(1, steps + 1):
        parts = [part] + [from_y(part, d) for d in (1, 3, 2)]
        if k == steps:
            (piece,) = small_call(last_step_kernel, place, parts, [], [piece_shape])
        else:
            solved, piece, part = small_call(
                step_kernel, place, parts + [rem[k]], both(low[(k, k - 1)]) + both(inv[k]),
                [x_shape, piece_shape, x_shape],
            )
            for later in range(k + 1, steps):
                (rem[later],) = small_call(ahead_kernel, None, [solved, rem[later]], both(low[(later, k - 1)]), [rem_shape])
        pieces.append(piece)

    def spread(two):
        return jnp.broadcast_to(jnp.stack(two)[None], (16, 2) + two[0].shape)

    def core_pairs(parts):
        out = []
        for part in parts:
            out += [part, from_core(part)]
        return out

    block = (inverses.shape[1], inverses.shape[2])
    def far_part(up, down):
        cut = up.shape[0] // 2
        return jnp.concatenate([from_y(up[:cut], 1), from_y(down[cut:], 3)])

    x_01 = lax.all_to_all(after(spread(pieces[0:2]), factor_01, pieces[3]), "col", 0, 0)
    up_01, down_01 = from_y(x_01, 1), from_y(x_01, 3)
    x_23 = lax.all_to_all(after(spread(pieces[2:4]), x_01), "col", 0, 0)
    factor_23 = lax.all_to_all(after(split_2, x_23, up_01, down_01), "col", 0, 0)
    across_01 = far_part(up_01, down_01)
    xs_01 = core_pairs([x_01, up_01, across_01, down_01])
    out, solved_0 = update(place, factor_01, 0, xs_01, 0, 2, trail_right, *block)
    x_23 = after(x_23, across_01)
    up_23, down_23 = from_y(x_23, 1), from_y(x_23, 3)
    across_23 = far_part(after(up_23, out), down_23)
    xs_23 = core_pairs([x_23, up_23, across_23, down_23])
    out, solved_2 = update(place, factor_23, 0, xs_23, 0, 2, out, *block)
    return (jnp.concatenate([solved_0, solved_2]), out)


def solution(mesh):
    in_specs = (
        P(None, "col", "row"),
        P(None, "col", "row"),
        P(None, "row", None),
        P(None, "col", "row"),
        P(("row", "col"), None),
    )
    out_specs = (P(None, "col", "row"), P(("row", "col"), None))
    return jax.shard_map(
        per_device, mesh=mesh, in_specs=in_specs, out_specs=out_specs, check_vma=False
    )
```

```python
import jax
import jax.numpy as jnp
from jax import lax
from jax.experimental import pallas as pl
from jax.experimental.pallas import tpu as pltpu
from jax.sharding import PartitionSpec as P

F32 = jnp.float32
BF16 = jnp.bfloat16


def col_perm(dx, dz):
    return [(((x + dx) % 4) * 4 + (z + dz) % 4, x * 4 + z) for x in range(4) for z in range(4)]


def y_perm(dy):
    return [(2 * ((y + dy) % 4) + c, 2 * y + c) for y in range(4) for c in range(2)]


CORE_PERM = [(i, i ^ 1) for i in range(8)]


def from_x(value, d):
    return lax.ppermute(value, "col", col_perm(d, 0))


def from_z(value, d):
    return lax.ppermute(value, "col", col_perm(0, d))


def from_y(value, d):
    return lax.ppermute(value, "row", y_perm(d))


def from_core(value):
    return lax.ppermute(value, "row", CORE_PERM)


def ring_stack(value, fetch):
    far = {d: fetch(value, d) for d in (1, 3, 2)}
    return jnp.stack([value, far[1], far[2], far[3]])


def gather_blocks(set_a, set_b, *others):
    near_a = ring_stack(set_a, from_x)
    near_b = ring_stack(set_b, from_z)
    near_a, near_b, *others = lax.optimization_barrier((near_a, near_b) + others)
    all_a = jnp.swapaxes(ring_stack(near_a, from_z), 0, 1)
    all_b = ring_stack(near_b, from_x)
    return all_a.reshape((-1,) + set_a.shape), all_b.reshape((-1,) + set_b.shape), *others


def split_bf16(value):
    high = value.astype(BF16)
    low = (value - high.astype(F32)).astype(BF16)
    return high, low


def dot3(a, b, dims):
    ah, al = split_bf16(a)
    bh, bl = split_bf16(b)

    def one(p, q):
        return lax.dot_general(p, q, (dims, ((), ())), preferred_element_type=F32)

    return one(ah, bh) + (one(ah, bl) + one(al, bh))


def dot_nn(a, b):
    return dot3(a, b, ((1,), (0,)))


def dot_nt(a, b):
    return dot3(a, b, ((1,), (1,)))


def flat(ref):
    value = ref[:, 0]
    return value.reshape(value.shape[0] * value.shape[1], value.shape[2])


def take_piece(place_ref, piece_ref, total):
    x, y, z = place_ref[0], place_ref[1], place_ref[2]
    width = piece_ref.shape[1]
    shift = lax.rem(y - x + 4, 4)
    quarter = total[:, 0:width]
    for d in range(1, 4):
        quarter = jnp.where(shift == d, total[:, d * width:(d + 1) * width], quarter)
    piece_ref[...] = pltpu.roll(quarter, z * (width // 4), 1)


def first_step_kernel(rem_ref, inv_own, inv_far, part_ref):
    half = inv_own.shape[3]
    rem = rem_ref[0]
    part_ref[...] = dot_nt(rem[:, :half], flat(inv_own)) + dot_nt(rem[:, half:], flat(inv_far))


def step_kernel(place_ref, p0, p1, p2, p3, rem_ref, low_own, low_far, inv_own, inv_far, x_ref, piece_ref, part_ref):
    half = inv_own.shape[3]
    total = (p0[...] + p1[...]) + (p2[...] + p3[...])
    x_ref[...] = total
    take_piece(place_ref, piece_ref, total)
    rem = rem_ref[0]
    left = rem[:, :half] - dot_nn(total, flat(low_own))
    right = rem[:, half:] - dot_nn(total, flat(low_far))
    part_ref[...] = dot_nt(left, flat(inv_own)) + dot_nt(right, flat(inv_far))


def last_step_kernel(place_ref, p0, p1, p2, p3, piece_ref):
    take_piece(place_ref, piece_ref, (p0[...] + p1[...]) + (p2[...] + p3[...]))


def ahead_kernel(x_ref, rem_ref, low_own, low_far, o_ref):
    half = low_own.shape[3]
    total = x_ref[...]
    o_ref[0, :, :half] = rem_ref[0, :, :half] - dot_nn(total, flat(low_own))
    o_ref[0, :, half:] = rem_ref[0, :, half:] - dot_nn(total, flat(low_far))


def block_spec(place):
    where, index = place
    shape = where.shape
    return pl.BlockSpec((shape[0], 1) + shape[2:], lambda *_: (0, index, 0, 0))


def whole_spec(array):
    zeros = (0,) * len(array.shape)
    return pl.BlockSpec(array.shape, lambda *_: zeros)


def small_call(kernel, place, plain, blocks, outs):
    specs = [whole_spec(v) for v in plain] + [block_spec(v) for v in blocks]
    return pl.pallas_call(
        kernel,
        grid_spec=pltpu.PrefetchScalarGridSpec(
            num_scalar_prefetch=0 if place is None else 1,
            grid=(1,),
            in_specs=specs,
            out_specs=[whole_spec(v) for v in outs],
        ),
        out_shape=outs,
        compiler_params=pltpu.CompilerParams(vmem_limit_bytes=40 * 2**20),
    )(*([] if place is None else [place]), *plain, *[v[0] for v in blocks])


def split_kernel(f_ref, o_ref):
    parts = o_ref.shape[0]
    width = o_ref.shape[3]
    for d in range(parts):
        o_ref[d, 0] = f_ref[0, :, d * width:(d + 1) * width]


def split_by_owner(factor, first, count, owners):
    rows = factor.shape[1]
    width = factor.shape[2] // owners
    per = 4
    return pl.pallas_call(
        split_kernel,
        grid=(count, owners // per),
        in_specs=[pl.BlockSpec((1, rows, per * width), lambda k, g: (first + k, 0, g))],
        out_specs=pl.BlockSpec((per, 1, rows, width), lambda k, g: (g, k, 0, 0)),
        out_shape=jax.ShapeDtypeStruct((owners, count, rows, width), F32),
        compiler_params=pltpu.CompilerParams(vmem_limit_bytes=32 * 2**20),
    )(factor)


def dot_b(a, b):
    return lax.dot_general(a, b, (((1,), (1,)), ((), ())), preferred_element_type=F32)


def update_kernel(place_ref, f_ref, *refs):
    x_refs = refs[:8]
    base_ref, o_ref, s_ref, high_ref, low_ref = refs[8:]
    step = pl.program_id(0)
    x, y, z, core, row = [place_ref[i] for i in range(5)]
    half = o_ref.shape[1] // 2
    width = x_refs[0].shape[3]

    @pl.when(step == 0)
    def _():
        o_ref[...] = base_ref[...]

    for d in range(4):
        quarter = pl.ds(pl.multiple_of(lax.rem(y + d, 4) * width, width), width)
        for side in range(2):
            part = x_refs[2 * d + side][:, 0]
            part = part.reshape(part.shape[0] * part.shape[1], width)
            high, low = split_bf16(part)
            high_ref[side, :, quarter] = high
            low_ref[side, :, quarter] = low

    block = s_ref.shape[1]
    for d in range(4):
        for side in range(2):
            mine = (lax.rem(x - y + 4, 4) == d) & ((row // 4 == core) == (side == 0))

            @pl.when(mine)
            def _(part_ref=x_refs[2 * d + side]):
                part = part_ref[pl.ds(4 * lax.rem(row, 4), 4), 0]
                part = part.reshape(part.shape[0] * part.shape[1], width)
                part = pltpu.roll(part, lax.rem(4 - z, 4) * block, 1)
                s_ref[0] = part[:, :128].T[:block]

    f = f_ref[:, 0]
    f = f.reshape(f.shape[0] * f.shape[1], f.shape[2]).T
    fh, fl = split_bf16(f)
    for side in range(2):
        where = core if side == 0 else 1 - core
        cols = pl.ds(pl.multiple_of(where * half, half), half)
        xh = high_ref[side]
        o_ref[:, cols] -= dot_b(fh, xh) + (dot_b(fh, low_ref[side]) + dot_b(fl, xh))


def update(place, factor, f_first, xs, x_first, count, base, s_rows, s_cols):
    owners, _, rows, width = factor.shape
    _, _, q, m = xs[0].shape
    whole = pl.BlockSpec(base.shape, lambda k, p: (0, 0))
    grid_spec = pltpu.PrefetchScalarGridSpec(
        num_scalar_prefetch=1,
        grid=(count,),
        in_specs=[pl.BlockSpec((owners, 1, rows, width), lambda k, p: (0, f_first + k, 0, 0))]
        + [pl.BlockSpec((owners, 1, q, m), lambda k, p: (0, x_first + k, 0, 0))] * 8
        + [whole],
        out_specs=[whole, pl.BlockSpec((1, s_rows, s_cols), lambda k, p: (k, 0, 0))],
        scratch_shapes=[
            pltpu.VMEM((2, owners * q, 4 * m), BF16),
            pltpu.VMEM((2, owners * q, 4 * m), BF16),
        ],
    )
    return pl.pallas_call(
        update_kernel,
        grid_spec=grid_spec,
        out_shape=[
            jax.ShapeDtypeStruct(base.shape, F32),
            jax.ShapeDtypeStruct((count, s_rows, s_cols), F32),
        ],
        compiler_params=pltpu.CompilerParams(vmem_limit_bytes=56 * 2**20),
    )(place, factor, *xs, base)


def per_device(lower_blocks, inverses, panel_right, trail_factor, trail_right):
    row = lax.axis_index("row")
    col = lax.axis_index("col")
    y, core = row // 2, row % 2
    x, z = col // 4, col % 4

    place = jnp.stack([x, y, z, core, row]).astype(jnp.int32)
    steps = inverses.shape[0]
    order = inverses.shape[1] * 16
    q_all = panel_right.shape[2]
    share = q_all // 32

    def columns(which):
        return lax.dynamic_slice_in_dim(panel_right, which * (q_all // 2) + col * share, share, 2)

    right_own = jnp.swapaxes(columns(core), 1, 2)
    right_far = from_core(jnp.swapaxes(columns(1 - core), 1, 2))
    right = jnp.concatenate([right_own, right_far], axis=2)

    set_a = jnp.concatenate([inverses[0:1], lower_blocks[0:1], inverses[1:2], lower_blocks[1:3]])
    set_b = jnp.concatenate([inverses[2:4], lower_blocks[3:6]])
    split_0 = split_by_owner(trail_factor, 0, 2, 16)
    split_2 = split_by_owner(trail_factor, 2, 2, 16)
    got_a, got_b, right, split_0 = gather_blocks(set_a, set_b, right, split_0)
    far_a = from_core(got_a)
    far_b = from_core(got_b)
    inv = [(0, 0), (0, 2), (1, 0), (1, 1)]
    low = {(1, 0): (0, 1), (2, 0): (0, 3), (2, 1): (0, 4), (3, 0): (1, 2), (3, 1): (1, 3), (3, 2): (1, 4)}

    def both(where):
        pair = ((got_a, far_a), (got_b, far_b))[where[0]]
        return [(v, where[1]) for v in pair]

    def after(value, *earlier):
        return lax.optimization_barrier((value,) + earlier)[0]

    factor_01 = lax.all_to_all(after(split_0, got_a, got_b), "col", 0, 0)

    x_shape = jax.ShapeDtypeStruct((share, order), F32)
    piece_shape = jax.ShapeDtypeStruct((share, order // 4), F32)
    rem_shape = jax.ShapeDtypeStruct((1, share, right.shape[2]), F32)
    rem = [right[k:k + 1] for k in range(steps)]

    pieces = []
    (part,) = small_call(first_step_kernel, None, [rem[0]], both(inv[0]), [x_shape])
    for k in range(1, steps + 1):
        parts = [part] + [from_y(part, d) for d in (1, 3, 2)]
        if k == steps:
            (piece,) = small_call(last_step_kernel, place, parts, [], [piece_shape])
        else:
            solved, piece, part = small_call(
                step_kernel, place, parts + [rem[k]], both(low[(k, k - 1)]) + both(inv[k]),
                [x_shape, piece_shape, x_shape],
            )
            for later in range(k + 1, steps):
                (rem[later],) = small_call(ahead_kernel, None, [solved, rem[later]], both(low[(later, k - 1)]), [rem_shape])
        pieces.append(piece)

    def spread(two):
        return jnp.broadcast_to(jnp.stack(two)[None], (16, 2) + two[0].shape)

    def core_pairs(parts):
        out = []
        for part in parts:
            out += [part, from_core(part)]
        return out

    block = (inverses.shape[1], inverses.shape[2])
    def far_part(up, down):
        cut = up.shape[0] // 2
        return jnp.concatenate([from_y(up[:cut], 1), from_y(down[cut:], 3)])

    x_01 = lax.all_to_all(after(spread(pieces[0:2]), factor_01, pieces[3]), "col", 0, 0)
    up_01, down_01 = from_y(x_01, 1), from_y(x_01, 3)
    x_23 = lax.all_to_all(after(spread(pieces[2:4]), x_01), "col", 0, 0)
    factor_23 = lax.all_to_all(after(split_2, x_23, up_01, down_01), "col", 0, 0)
    across_01 = far_part(up_01, down_01)
    xs_01 = core_pairs([x_01, up_01, across_01, down_01])
    out, solved_0 = update(place, factor_01, 0, xs_01, 0, 2, trail_right, *block)
    up_23, down_23 = from_y(x_23, 1), from_y(x_23, 3)
    across_23 = far_part(after(up_23, out), down_23)
    xs_23 = core_pairs([x_23, up_23, across_23, down_23])
    out, solved_2 = update(place, factor_23, 0, xs_23, 0, 2, out, *block)
    return (jnp.concatenate([solved_0, solved_2]), out)


def solution(mesh):
    in_specs = (
        P(None, "col", "row"),
        P(None, "col", "row"),
        P(None, "row", None),
        P(None, "col", "row"),
        P(("row", "col"), None),
    )
    out_specs = (P(None, "col", "row"), P(("row", "col"), None))
    return jax.shard_map(
        per_device, mesh=mesh, in_specs=in_specs, out_specs=out_specs, check_vma=False
    )
```

```python
import jax
import jax.numpy as jnp
from jax import lax
from jax.experimental import pallas as pl
from jax.experimental.pallas import tpu as pltpu
from jax.sharding import PartitionSpec as P

F32 = jnp.float32
BF16 = jnp.bfloat16


def col_perm(dx, dz):
    return [(((x + dx) % 4) * 4 + (z + dz) % 4, x * 4 + z) for x in range(4) for z in range(4)]


def y_perm(dy):
    return [(2 * ((y + dy) % 4) + c, 2 * y + c) for y in range(4) for c in range(2)]


CORE_PERM = [(i, i ^ 1) for i in range(8)]


def from_x(value, d):
    return lax.ppermute(value, "col", col_perm(d, 0))


def from_z(value, d):
    return lax.ppermute(value, "col", col_perm(0, d))


def from_y(value, d):
    return lax.ppermute(value, "row", y_perm(d))


def from_core(value):
    return lax.ppermute(value, "row", CORE_PERM)


def ring_stack(value, fetch):
    far = {d: fetch(value, d) for d in (1, 3, 2)}
    return jnp.stack([value, far[1], far[2], far[3]])


def gather_blocks(set_a, set_b, prepare):
    near_a = ring_stack(set_a, from_x)
    near_b = ring_stack(set_b, from_z)
    near_a, near_b, *others = lax.optimization_barrier((near_a, near_b) + prepare(near_a))
    all_a = jnp.swapaxes(ring_stack(near_a, from_z), 0, 1)
    all_b = ring_stack(near_b, from_x)
    return all_a.reshape((-1,) + set_a.shape), all_b.reshape((-1,) + set_b.shape), *others


def split_bf16(value):
    high = value.astype(BF16)
    low = (value - high.astype(F32)).astype(BF16)
    return high, low


def dot3(a, b, dims):
    ah, al = split_bf16(a)
    bh, bl = split_bf16(b)

    def one(p, q):
        return lax.dot_general(p, q, (dims, ((), ())), preferred_element_type=F32)

    return one(ah, bh) + (one(ah, bl) + one(al, bh))


def dot_nn(a, b):
    return dot3(a, b, ((1,), (0,)))


def dot_nt(a, b):
    return dot3(a, b, ((1,), (1,)))


def flat(ref):
    value = ref[:, 0]
    return value.reshape(value.shape[0] * value.shape[1], value.shape[2])


def take_piece(place_ref, piece_ref, total):
    x, y, z = place_ref[0], place_ref[1], place_ref[2]
    width = piece_ref.shape[1]
    shift = lax.rem(y - x + 4, 4)
    quarter = total[:, 0:width]
    for d in range(1, 4):
        quarter = jnp.where(shift == d, total[:, d * width:(d + 1) * width], quarter)
    piece_ref[...] = pltpu.roll(quarter, z * (width // 4), 1)


def first_step_kernel(rem_ref, inv_own, inv_far, part_ref):
    half = inv_own.shape[3]
    rem = rem_ref[0]
    part_ref[...] = dot_nt(rem[:, :half], flat(inv_own)) + dot_nt(rem[:, half:], flat(inv_far))


def step_kernel(place_ref, p0, p1, p2, p3, rem_ref, low_own, low_far, inv_own, inv_far, x_ref, piece_ref, part_ref):
    half = inv_own.shape[3]
    total = (p0[...] + p1[...]) + (p2[...] + p3[...])
    x_ref[...] = total
    take_piece(place_ref, piece_ref, total)
    rem = rem_ref[0]
    left = rem[:, :half] - dot_nn(total, flat(low_own))
    right = rem[:, half:] - dot_nn(total, flat(low_far))
    part_ref[...] = dot_nt(left, flat(inv_own)) + dot_nt(right, flat(inv_far))


def last_step_kernel(place_ref, p0, p1, p2, p3, piece_ref):
    take_piece(place_ref, piece_ref, (p0[...] + p1[...]) + (p2[...] + p3[...]))


def ahead_kernel(x_ref, rem_ref, low_own, low_far, o_ref):
    half = low_own.shape[3]
    total = x_ref[...]
    o_ref[0, :, :half] = rem_ref[0, :, :half] - dot_nn(total, flat(low_own))
    o_ref[0, :, half:] = rem_ref[0, :, half:] - dot_nn(total, flat(low_far))


def block_spec(place):
    where, index = place
    shape = where.shape
    return pl.BlockSpec((shape[0], 1) + shape[2:], lambda *_: (0, index, 0, 0))


def whole_spec(array):
    zeros = (0,) * len(array.shape)
    return pl.BlockSpec(array.shape, lambda *_: zeros)


def small_call(kernel, place, plain, blocks, outs):
    specs = [whole_spec(v) for v in plain] + [block_spec(v) for v in blocks]
    return pl.pallas_call(
        kernel,
        grid_spec=pltpu.PrefetchScalarGridSpec(
            num_scalar_prefetch=0 if place is None else 1,
            grid=(1,),
            in_specs=specs,
            out_specs=[whole_spec(v) for v in outs],
        ),
        out_shape=outs,
        compiler_params=pltpu.CompilerParams(vmem_limit_bytes=40 * 2**20),
    )(*([] if place is None else [place]), *plain, *[v[0] for v in blocks])


def split_kernel(f_ref, o_ref):
    parts = o_ref.shape[0]
    width = o_ref.shape[3]
    for d in range(parts):
        o_ref[d, 0] = f_ref[0, :, d * width:(d + 1) * width]


def split_by_owner(factor, first, count, owners):
    rows = factor.shape[1]
    width = factor.shape[2] // owners
    per = 4
    return pl.pallas_call(
        split_kernel,
        grid=(count, owners // per),
        in_specs=[pl.BlockSpec((1, rows, per * width), lambda k, g: (first + k, 0, g))],
        out_specs=pl.BlockSpec((per, 1, rows, width), lambda k, g: (g, k, 0, 0)),
        out_shape=jax.ShapeDtypeStruct((owners, count, rows, width), F32),
        compiler_params=pltpu.CompilerParams(vmem_limit_bytes=32 * 2**20),
    )(factor)


def dot_b(a, b):
    return lax.dot_general(a, b, (((1,), (1,)), ((), ())), preferred_element_type=F32)


def update_kernel(place_ref, f_ref, *refs):
    x_refs = refs[:8]
    base_ref, o_ref, s_ref, high_ref, low_ref = refs[8:]
    step = pl.program_id(0)
    x, y, z, core, row = [place_ref[i] for i in range(5)]
    half = o_ref.shape[1] // 2
    width = x_refs[0].shape[3]

    @pl.when(step == 0)
    def _():
        o_ref[...] = base_ref[...]

    for d in range(4):
        quarter = pl.ds(pl.multiple_of(lax.rem(y + d, 4) * width, width), width)
        for side in range(2):
            part = x_refs[2 * d + side][:, 0]
            part = part.reshape(part.shape[0] * part.shape[1], width)
            high, low = split_bf16(part)
            high_ref[side, :, quarter] = high
            low_ref[side, :, quarter] = low

    block = s_ref.shape[1]
    for d in range(4):
        for side in range(2):
            mine = (lax.rem(x - y + 4, 4) == d) & ((row // 4 == core) == (side == 0))

            @pl.when(mine)
            def _(part_ref=x_refs[2 * d + side]):
                part = part_ref[pl.ds(4 * lax.rem(row, 4), 4), 0]
                part = part.reshape(part.shape[0] * part.shape[1], width)
                part = pltpu.roll(part, lax.rem(4 - z, 4) * block, 1)
                s_ref[0] = part[:, :128].T[:block]

    f = f_ref[:, 0]
    f = f.reshape(f.shape[0] * f.shape[1], f.shape[2]).T
    fh, fl = split_bf16(f)
    for side in range(2):
        where = core if side == 0 else 1 - core
        cols = pl.ds(pl.multiple_of(where * half, half), half)
        xh = high_ref[side]
        o_ref[:, cols] -= dot_b(fh, xh) + (dot_b(fh, low_ref[side]) + dot_b(fl, xh))


def update(place, factor, f_first, xs, x_first, count, base, s_rows, s_cols):
    owners, _, rows, width = factor.shape
    _, _, q, m = xs[0].shape
    whole = pl.BlockSpec(base.shape, lambda k, p: (0, 0))
    grid_spec = pltpu.PrefetchScalarGridSpec(
        num_scalar_prefetch=1,
        grid=(count,),
        in_specs=[pl.BlockSpec((owners, 1, rows, width), lambda k, p: (0, f_first + k, 0, 0))]
        + [pl.BlockSpec((owners, 1, q, m), lambda k, p: (0, x_first + k, 0, 0))] * 8
        + [whole],
        out_specs=[whole, pl.BlockSpec((1, s_rows, s_cols), lambda k, p: (k, 0, 0))],
        scratch_shapes=[
            pltpu.VMEM((2, owners * q, 4 * m), BF16),
            pltpu.VMEM((2, owners * q, 4 * m), BF16),
        ],
    )
    return pl.pallas_call(
        update_kernel,
        grid_spec=grid_spec,
        out_shape=[
            jax.ShapeDtypeStruct(base.shape, F32),
            jax.ShapeDtypeStruct((count, s_rows, s_cols), F32),
        ],
        compiler_params=pltpu.CompilerParams(vmem_limit_bytes=56 * 2**20),
    )(place, factor, *xs, base)


def per_device(lower_blocks, inverses, panel_right, trail_factor, trail_right):
    row = lax.axis_index("row")
    col = lax.axis_index("col")
    y, core = row // 2, row % 2
    x, z = col // 4, col % 4

    place = jnp.stack([x, y, z, core, row]).astype(jnp.int32)
    steps = inverses.shape[0]
    order = inverses.shape[1] * 16
    q_all = panel_right.shape[2]
    share = q_all // 32

    def columns(which):
        return lax.dynamic_slice_in_dim(panel_right, which * (q_all // 2) + col * share, share, 2)

    right_own = jnp.swapaxes(columns(core), 1, 2)
    right_far = from_core(jnp.swapaxes(columns(1 - core), 1, 2))
    right = jnp.concatenate([right_own, right_far], axis=2)

    set_a = jnp.concatenate([inverses[0:1], lower_blocks[0:1], inverses[1:2], lower_blocks[1:3]])
    set_b = jnp.concatenate([inverses[2:4], lower_blocks[3:6]])

    def prepare(near):
        factor = lax.optimization_barrier((trail_factor, near))[0]
        return right, split_by_owner(factor, 0, 2, 16)

    split_2 = split_by_owner(trail_factor, 2, 2, 16)
    got_a, got_b, right, split_0 = gather_blocks(set_a, set_b, prepare)
    far_a = from_core(got_a)
    far_b = from_core(got_b)
    inv = [(0, 0), (0, 2), (1, 0), (1, 1)]
    low = {(1, 0): (0, 1), (2, 0): (0, 3), (2, 1): (0, 4), (3, 0): (1, 2), (3, 1): (1, 3), (3, 2): (1, 4)}

    def both(where):
        pair = ((got_a, far_a), (got_b, far_b))[where[0]]
        return [(v, where[1]) for v in pair]

    def after(value, *earlier):
        return lax.optimization_barrier((value,) + earlier)[0]

    factor_01 = lax.all_to_all(after(split_0, got_a, got_b), "col", 0, 0)

    x_shape = jax.ShapeDtypeStruct((share, order), F32)
    piece_shape = jax.ShapeDtypeStruct((share, order // 4), F32)
    rem_shape = jax.ShapeDtypeStruct((1, share, right.shape[2]), F32)
    rem = [right[k:k + 1] for k in range(steps)]

    pieces = []
    (part,) = small_call(first_step_kernel, None, [rem[0]], both(inv[0]), [x_shape])
    for k in range(1, steps + 1):
        parts = [part] + [from_y(part, d) for d in (1, 3, 2)]
        if k == steps:
            (piece,) = small_call(last_step_kernel, place, parts, [], [piece_shape])
        else:
            solved, piece, part = small_call(
                step_kernel, place, parts + [rem[k]], both(low[(k, k - 1)]) + both(inv[k]),
                [x_shape, piece_shape, x_shape],
            )
            for later in range(k + 1, steps):
                (rem[later],) = small_call(ahead_kernel, None, [solved, rem[later]], both(low[(later, k - 1)]), [rem_shape])
        pieces.append(piece)

    def spread(two):
        return jnp.broadcast_to(jnp.stack(two)[None], (16, 2) + two[0].shape)

    def core_pairs(parts):
        out = []
        for part in parts:
            out += [part, from_core(part)]
        return out

    block = (inverses.shape[1], inverses.shape[2])
    def far_part(up, down):
        cut = up.shape[0] // 2
        return jnp.concatenate([from_y(up[:cut], 1), from_y(down[cut:], 3)])

    x_01 = lax.all_to_all(after(spread(pieces[0:2]), factor_01, pieces[3]), "col", 0, 0)
    up_01, down_01 = from_y(x_01, 1), from_y(x_01, 3)
    x_23 = lax.all_to_all(after(spread(pieces[2:4]), x_01), "col", 0, 0)
    factor_23 = lax.all_to_all(after(split_2, x_23, up_01, down_01), "col", 0, 0)
    across_01 = far_part(up_01, down_01)
    xs_01 = core_pairs([x_01, up_01, across_01, down_01])
    out, solved_0 = update(place, factor_01, 0, xs_01, 0, 2, trail_right, *block)
    x_23 = after(x_23, across_01)
    up_23, down_23 = from_y(x_23, 1), from_y(x_23, 3)
    across_23 = far_part(after(up_23, out), down_23)
    xs_23 = core_pairs([x_23, up_23, across_23, down_23])
    out, solved_2 = update(place, factor_23, 0, xs_23, 0, 2, out, *block)
    return (jnp.concatenate([solved_0, solved_2]), out)


def solution(mesh):
    in_specs = (
        P(None, "col", "row"),
        P(None, "col", "row"),
        P(None, "row", None),
        P(None, "col", "row"),
        P(("row", "col"), None),
    )
    out_specs = (P(None, "col", "row"), P(("row", "col"), None))
    return jax.shard_map(
        per_device, mesh=mesh, in_specs=in_specs, out_specs=out_specs, check_vma=False
    )
```
